256 devices in a mesh: wide: 128 (over y, x_hi, z, core), narrow: 2 (over x_lo).
Axes of the slice: x: 4 (x_hi: 2, x_lo: 2; x = x_hi * 2 + x_lo), y: 4, z: 8, core: 2. Of those that a mesh axis runs over, the one named last changes fastest.
Arguments:
- positions: float32 [3, 65536], P(None, 'wide'), may hold values from -6 to 6
- velocities: float32 [3, 65536], P(None, 'wide'), may hold values from -6 to 6
- accelerations: float32 [3, 65536], P(None, 'wide'), may hold values from -6 to 6
- jerks: float32 [3, 65536], P(None, 'wide'), may hold values from -6 to 6
- snaps: float32 [3, 65536], P(None, 'wide'), may hold values from -36 to 36
- masses: float32 [65536], P('wide'), may hold values from 0.5 to 2
Outputs:
- new_positions: float32 [3, 65536], P(None, 'wide')
- new_velocities: float32 [3, 65536], P(None, 'wide')
- new_accelerations: float32 [3, 65536], P(None, 'wide')
- new_jerks: float32 [3, 65536], P(None, 'wide')
- new_snaps: float32 [3, 65536], P(None, 'wide')
- crackle_step: float32 [3, 65536], P(None, 'wide')
The draws below stay inside these ranges and needn't reach their ends.
All inputs are finite; a program needn't handle non-finite values.
Results may differ from the reference program's by a relative error of at most 0.00026.
Values sent between devices are 32-bit elements; how exact they have to be, the bound alone decides.
A program may use at most 64 MiB of HBM per device.

```python
import math
import jax
import jax.numpy as jnp
from jax import lax

TGT_DEV = 512
STARS = 65536
N_WIDE = 128


def levels(own_key, dims, pieces, low, high):
    factor_of, own = 1.0, jax.random.fold_in(own_key, 6)
    for dim, blocks in pieces:
        draws = jnp.exp(jax.random.uniform(jax.random.fold_in(own, dim), (blocks,), jnp.float32, low / len(pieces), high / len(pieces)))
        factor_of = factor_of * jnp.repeat(draws, dims[dim] // blocks).reshape([-1 if axis == dim else 1 for axis in range(len(dims))])
    return factor_of


def bell_draw(stream_key, shape, width, most, pieces=(), kind=jnp.bfloat16):
    values = width * jax.random.normal(stream_key, shape, jnp.float32)
    if pieces:
        values = values * levels(stream_key, shape, pieces, -0.22, 0.18)
    return jnp.clip(values, -most, most).astype(kind)


def setup_inputs(seed: int = 0) -> dict:
    streams_of = jax.random.split(jax.random.key(seed), 7)
    positions = bell_draw(streams_of[0], (3, STARS), 1.0, 6.0, ((1, 128),), jnp.float32)
    velocities = bell_draw(streams_of[1], (3, STARS), 0.5, 6.0, ((1, 128),), jnp.float32)
    accelerations = bell_draw(streams_of[2], (3, STARS), 1.0, 6.0, ((1, 128),), jnp.float32)
    jerks = bell_draw(streams_of[3], (3, STARS), 1.0, 6.0, ((1, 128),), jnp.float32)
    snaps = bell_draw(streams_of[4], (3, STARS), 6.0, 36.0, ((1, 128),), jnp.float32)
    masses = jnp.clip(jnp.exp(math.log(2.0) - 1.3862944 * jax.random.uniform(streams_of[5], (STARS,), jnp.float32) ** levels(streams_of[5], (STARS,), ((0, 128),), -0.2, 0.2)), 0.5, 2.0)
    return dict(positions=positions, velocities=velocities, accelerations=accelerations, jerks=jerks, snaps=snaps, masses=masses)


softening = 0.01
time_step = 0.0625

def predict(positions, velocities, accelerations, jerks, snaps):
    h = time_step
    pred_x = positions + h * velocities + h * h / 2.0 * accelerations + h ** 3 / 6.0 * jerks + h ** 4 / 24.0 * snaps
    pred_v = velocities + h * accelerations + h * h / 2.0 * jerks + h ** 3 / 6.0 * snaps
    pred_a = accelerations + h * jerks + h * h / 2.0 * snaps
    return (pred_x, pred_v, pred_a)

def pair_forces(targets, sources):
    separation = sources[0:3, None, :] - targets[0:3, :, None]
    relative_vel = sources[3:6, None, :] - targets[3:6, :, None]
    relative_acc = sources[6:9, None, :] - targets[6:9, :, None]
    dist_sq = lax.optimization_barrier(jnp.sum(separation * separation, axis=0)) + softening
    inverse_sq = 1.0 / dist_sq
    strength = sources[9][None, :] * inverse_sq * jnp.sqrt(inverse_sq)
    radial = lax.optimization_barrier(jnp.sum(separation * relative_vel, axis=0)) * inverse_sq
    curving = (lax.optimization_barrier(jnp.sum(relative_vel * relative_vel, axis=0)) + lax.optimization_barrier(jnp.sum(separation * relative_acc, axis=0))) * inverse_sq + radial * radial
    accel_pair = strength * separation
    jerk_pair = strength * relative_vel - 3.0 * radial * accel_pair
    snap_pair = strength * relative_acc - 6.0 * radial * jerk_pair - 3.0 * curving * accel_pair
    return jnp.concatenate([lax.optimization_barrier(jnp.sum(accel_pair, axis=-1)), lax.optimization_barrier(jnp.sum(jerk_pair, axis=-1)), lax.optimization_barrier(jnp.sum(snap_pair, axis=-1))], axis=0)

def correct(positions, velocities, accelerations, jerks, snaps, forces):
    h = time_step
    new_acc = forces[0:3]
    new_jerk = forces[3:6]
    new_snap = forces[6:9]
    new_vel = velocities + h / 2.0 * (new_acc + accelerations) - h * h / 10.0 * (new_jerk - jerks) + h ** 3 / 120.0 * (new_snap + snaps)
    new_pos = positions + h / 2.0 * (new_vel + velocities) - h * h / 10.0 * (new_acc - accelerations) + h ** 3 / 120.0 * (new_jerk + jerks)
    first = new_acc - accelerations - h * jerks - h * h / 2.0 * snaps
    second = h * (new_jerk - jerks - h * snaps)
    third = h * h * (new_snap - snaps)
    crackle = 60.0 * first - 36.0 * second + 9.0 * third
    return (new_pos, new_vel, new_acc, new_jerk, new_snap, crackle)

def reference(positions, velocities, accelerations, jerks, snaps, masses):
    pred_x, pred_v, pred_a = predict(positions, velocities, accelerations, jerks, snaps)
    source = jnp.concatenate([pred_x, pred_v, pred_a, (masses / STARS)[None, :]], axis=0)
    block_size = math.gcd(STARS, 4096)
    source_blocks = source.reshape(10, STARS // block_size, block_size).transpose(1, 0, 2)
    target_blocks = source[0:9].reshape(9, N_WIDE, TGT_DEV).transpose(1, 0, 2)

    def one_target_block(targets):

        def add_block(carry, block):
            return (carry + pair_forces(targets, block), None)
        total, _ = lax.scan(add_block, jnp.zeros((9, TGT_DEV), jnp.float32), source_blocks)
        return total
    forces = lax.map(one_target_block, target_blocks)
    forces = forces.transpose(1, 0, 2).reshape(9, STARS)
    return correct(positions, velocities, accelerations, jerks, snaps, forces)
```

```python
import functools

import jax
import jax.numpy as jnp
from jax import lax
from jax.experimental import pallas as pl
from jax.experimental.pallas import tpu as pltpu
from jax.sharding import PartitionSpec as P

softening = 0.01
time_step = 0.0625

bf16 = jnp.bfloat16
f32 = jnp.float32
f8 = jnp.float8_e4m3fn
MESH = pl.DeviceIdType.MESH

CORES, NZ, NX, NY = 2, 8, 2, 4
BLOCKS = CORES * NZ * NX * NY
CHUNK = 2
PARTS = 2
STEP = CHUNK * PARTS
TILE = 256

Q_SCALE = 2.0**-4
P_SCALE = 2.0**-10.5
G_SCALE = 0.2 * 2.0**-17
W_BACK = 2.0**-6
C1_BACK = 2.0**0.5
C2_BACK = 2.0**7


def predict(positions, velocities, accelerations, jerks, snaps):
    pred_x = (
        positions
        + time_step * velocities
        + time_step * time_step / 2.0 * accelerations
        + time_step**3 / 6.0 * jerks
        + time_step**4 / 24.0 * snaps
    )
    pred_v = (
        velocities
        + time_step * accelerations
        + time_step * time_step / 2.0 * jerks
        + time_step**3 / 6.0 * snaps
    )
    pred_a = accelerations + time_step * jerks + time_step * time_step / 2.0 * snaps
    return (pred_x, pred_v, pred_a)


def correct(positions, velocities, accelerations, jerks, snaps, forces):
    new_acc = forces[0:3]
    new_jerk = forces[3:6]
    new_snap = forces[6:9]
    new_vel = (
        velocities
        + time_step / 2.0 * (new_acc + accelerations)
        - time_step * time_step / 10.0 * (new_jerk - jerks)
        + time_step**3 / 120.0 * (new_snap + snaps)
    )
    new_pos = (
        positions
        + time_step / 2.0 * (new_vel + velocities)
        - time_step * time_step / 10.0 * (new_acc - accelerations)
        + time_step**3 / 120.0 * (new_jerk + jerks)
    )
    first = new_acc - accelerations - time_step * jerks - time_step * time_step / 2.0 * snaps
    second = time_step * (new_jerk - jerks - time_step * snaps)
    third = time_step * time_step * (new_snap - snaps)
    crackle = 60.0 * first - 36.0 * second + 9.0 * third
    return (new_pos, new_vel, new_acc, new_jerk, new_snap, crackle)


def transfers():
    plan = []

    def put(step, to, src, dst, count=1):
        plan.append((step, to, src, dst, count))

    for to, dst in (("core", 1), ("z+", 2), ("z-", 3), ("y+", 4), ("y-", 5), ("x", 17)):
        put(-1, to, 0, dst)
    put(0, "z+", 2, 8)
    put(0, "z-", 3, 9)
    put(0, "core", 2, 6, 2)
    put(0, "y+", 2, 19, 2)
    put(0, "y-", 2, 34, 2)
    put(0, "x", 2, 65, 2)
    put(0, "core", 4, 26)
    put(0, "core", 5, 41)
    put(0, "y+", 4, 49)
    put(0, "x", 4, 80)
    put(0, "x", 5, 96)
    put(1, "z+", 8, 12)
    put(1, "z-", 9, 13)
    put(1, "core", 8, 10, 2)
    put(1, "y+", 8, 21, 2)
    put(1, "y-", 8, 36, 2)
    put(1, "x", 8, 67, 2)
    put(2, "z+", 12, 16)
    put(2, "core", 12, 14, 2)
    put(2, "y+", 12, 23, 2)
    put(2, "y-", 12, 38, 2)
    put(2, "x", 12, 69, 2)
    put(3, "core", 16, 18)
    put(3, "y+", 16, 25)
    put(3, "y-", 16, 40)
    put(3, "x", 16, 71)
    put(3, "core", 17, 72)
    put(4, "y+", 19, 50, 3)
    put(5, "core", 19, 27, 7)
    put(5, "x", 19, 81, 7)
    put(5, "y-", 37, 53, 4)
    put(5, "core", 34, 42, 7)
    put(5, "x", 34, 97, 7)
    put(8, "core", 49, 57, 8)
    put(8, "x", 49, 112, 8)
    put(12, "core", 65, 73, 7)
    put(14, "core", 80, 88, 8)
    put(16, "core", 96, 104, 8)
    put(18, "core", 112, 120, 8)
    return plan


def waits(plan):
    due = []
    for _, _, _, dst, count in plan:
        use = max(-1, -((5 - dst) // STEP))
        for step, _, src, _, length in plan:
            if src < dst + count and dst < src + length:
                use = min(use, step)
        due.append(use)
    return due


def split3(value):
    high = value.astype(bf16)
    rest = value - high.astype(f32)
    middle = rest.astype(bf16)
    low = (rest - middle.astype(f32)).astype(bf16)
    return high, middle, low


def product(left, right, over_left):
    return lax.dot_general(
        left, right, (((over_left,), (0,)), ((), ())), preferred_element_type=f32
    )


def source_rows(block):
    high, middle, low = split3(block)
    return jnp.concatenate([high, high, high, middle, middle, low], axis=0)


def sum_rows(block):
    weighed = block * block[12:13]
    fine = jnp.concatenate(split3(weighed), axis=0)
    high = weighed.astype(f8)
    rest = (weighed - high.astype(f32)).astype(f8)
    coarse = jnp.concatenate([high.astype(f32), rest.astype(f32)], axis=0).astype(f8)
    return fine, coarse


def forces_kernel(
    pos_ref, vel_ref, acc_ref, jerk_ref, snap_ref, mass_ref, out_ref,
    slots, own, feature, weights, pairs, total, total_low, part, other,
    send_sem, recv_sem, narrow_sem,
):
    wide, narrow = lax.axis_index("wide"), lax.axis_index("narrow")
    core, z = wide % CORES, (wide // CORES) % NZ
    x, y = (wide // (CORES * NZ)) % NX, wide // (CORES * NZ * NX)

    def index(y, x, z, core):
        return ((y * NX + x) * NZ + z) * CORES + core

    partner = {
        "core": {"wide": index(y, x, z, 1 - core)},
        "z+": {"wide": index(y, x, (z + 1) % NZ, core)},
        "z-": {"wide": index(y, x, (z + NZ - 1) % NZ, core)},
        "y+": {"wide": index((y + 1) % NY, x, z, core)},
        "y-": {"wide": index((y + NY - 1) % NY, x, z, core)},
        "x": {"wide": index(y, 1 - x, z, core)},
        "narrow": {"narrow": 1 - narrow},
    }
    barrier = pltpu.get_barrier_semaphore()
    for device in partner.values():
        pl.semaphore_signal(barrier, inc=1, device_id=device, device_id_type=MESH)

    star_x, star_v, star_a = predict(
        pos_ref[...], vel_ref[...], acc_ref[...], jerk_ref[...], snap_ref[...]
    )
    targets = star_x.shape[1]
    half = targets // 2
    xx = jnp.sum(star_x * star_x, axis=0, keepdims=True)
    xv = jnp.sum(star_x * star_v, axis=0, keepdims=True)
    vv = jnp.sum(star_v * star_v, axis=0, keepdims=True) + jnp.sum(
        star_x * star_a, axis=0, keepdims=True
    )
    one = jnp.ones_like(xx)
    own[...] = jnp.zeros_like(own)
    for row, value in (
        (0, star_x), (3, star_v), (6, star_a), (9, xx), (10, xv), (11, vv),
        (12, mass_ref[...]), (13, one),
    ):
        own[row : row + value.shape[0], :] = value
    start = pl.multiple_of(narrow * half, half)
    slots[0] = own[:, pl.ds(start, half)]
    pl.semaphore_wait(barrier, len(partner))

    plan = transfers()
    due = waits(plan)

    def copy(number):
        _, to, src, dst, count = plan[number]
        return pltpu.make_async_remote_copy(
            src_ref=slots.at[pl.ds(src, count)],
            dst_ref=slots.at[pl.ds(dst, count)],
            send_sem=send_sem.at[number],
            recv_sem=recv_sem.at[number],
            device_id=partner[to],
            device_id_type=MESH,
        )

    def exchange(step):
        for number in range(len(plan)):
            if due[number] == step and plan[number][0] < step:
                copy(number).wait_recv()
        for number in range(len(plan)):
            if plan[number][0] == step:
                copy(number).start()
        for number in range(len(plan)):
            if due[number] == step and plan[number][0] >= step:
                copy(number).wait_recv()

    for number in range(len(plan)):
        if plan[number][0] == -1:
            copy(number).start()

    feature[...] = jnp.zeros_like(feature)
    for kind, rows in enumerate((
        ((0, -2.0 * Q_SCALE * star_x), (9, Q_SCALE * one), (13, Q_SCALE * (xx + softening))),
        ((0, -P_SCALE * star_v), (3, -P_SCALE * star_x), (10, P_SCALE * one), (13, P_SCALE * xv)),
        (
            (0, -G_SCALE * star_a), (3, -2.0 * G_SCALE * star_v), (6, -G_SCALE * star_x),
            (11, G_SCALE * one), (13, G_SCALE * vv),
        ),
    )):
        for row, value in rows:
            feature[kind, row : row + value.shape[0], :] = value
        high, middle, low = split3(feature[kind])
        weights[kind] = jnp.concatenate([high, middle, low, high, middle, high], axis=0)

    total[...] = jnp.zeros_like(total)
    total_low[...] = jnp.zeros_like(total_low)

    def chunk_of(number):
        return jnp.concatenate([slots[number * CHUNK + u] for u in range(CHUNK)], axis=1)

    def forward(rows, parity, kind, tile):
        columns = slice(tile * TILE, (tile + 1) * TILE)
        pairs[parity, kind, :, columns] = product(rows, weights[kind, :, columns], 0)

    for number in range(len(plan)):
        if plan[number][0] == -1 and due[number] == -1:
            copy(number).wait_recv()
    rows = source_rows(chunk_of(0))
    for kind in range(3):
        for tile in range(targets // TILE):
            forward(rows, 0, kind, tile)

    steps = BLOCKS // STEP
    events = sorted(set([d for d in due if d >= 0] + [t[0] for t in plan if t[0] >= 0]))

    def branch(step, numbers):
        if len(numbers) <= 2:
            for number in numbers:
                pl.when(step == number)(functools.partial(exchange, number))
            return
        middle = len(numbers) // 2
        first, second = numbers[:middle], numbers[middle:]
        pl.when(step < second[0])(functools.partial(branch, step, first))
        pl.when(step >= second[0])(functools.partial(branch, step, second))

    def body(step, carry):
        branch(step, events)
        for parity in range(PARTS):
            chunk = step * PARTS + parity
            now, later = parity % 2, (parity + 1) % 2
            fine, coarse = sum_rows(chunk_of(chunk))
            ahead = source_rows(chunk_of(lax.min(chunk + 1, BLOCKS // CHUNK - 1)))
            work = [(kind, tile) for kind in range(3) for tile in range(targets // TILE)]
            units = [(b, tile) for b in range(CHUNK) for tile in range(targets // TILE)]
            done = 0
            for place, (b, tile) in enumerate(units):
                js = slice(b * half, (b + 1) * half)
                columns = slice(tile * TILE, (tile + 1) * TILE)
                q, p, g = [pairs[now, kind, js, columns] for kind in range(3)]
                root = lax.rsqrt(q)
                inverse = root * root
                w = inverse * root
                radial = p * inverse
                c1 = radial * w
                c2 = (w * inverse) * (p * radial - g)
                for kind, value in enumerate((w, c1, c2)):
                    high = value.astype(bf16)
                    low = (value - high.astype(f32)).astype(f8)
                    total[kind, :, columns] += product(fine[:, js], high, 1)
                    total_low[kind, :, columns] += product(coarse[:, js], low, 1)
                until = (place + 1) * len(work) // len(units)
                for kind, at in work[done:until]:
                    forward(ahead, later, kind, at)
                done = until
        return carry

    lax.fori_loop(0, steps, body, 0)

    sums = []
    for kind in range(3):
        sums.append(
            total[kind, 0:16] + total[kind, 16:32] + total[kind, 32:48]
            + total_low[kind, 0:16] + total_low[kind, 16:32]
        )
    sw, s1, s2 = sums
    share = 1.0 / (targets * BLOCKS)
    star_x, star_v, star_a = own[0:3, :], own[3:6, :], own[6:9, :]
    part[...] = jnp.zeros_like(part)
    part[0:3, :] = (W_BACK * share) * (sw[0:3] - star_x * sw[13:14])
    c1x = (C1_BACK * share) * (s1[0:3] - star_x * s1[13:14])
    part[3:6, :] = (W_BACK * share) * (sw[3:6] - star_v * sw[13:14]) - 3.0 * c1x
    part[6:9, :] = (
        (W_BACK * share) * (sw[6:9] - star_a * sw[13:14])
        - (6.0 * C1_BACK * share) * (s1[3:6] - star_v * s1[13:14])
        + (15.0 * C2_BACK * share) * (s2[0:3] - star_x * s2[13:14])
    )
    swap = pltpu.make_async_remote_copy(
        src_ref=part,
        dst_ref=other,
        send_sem=narrow_sem.at[0],
        recv_sem=narrow_sem.at[1],
        device_id=partner["narrow"],
        device_id_type=MESH,
    )
    swap.start()
    for number in range(len(plan)):
        copy(number).wait_send()
    swap.wait()
    out_ref[...] = part[...] + other[...]


def shards(positions, velocities, accelerations, jerks, snaps, masses):
    targets = positions.shape[1]
    half = targets // 2
    count = len(transfers())
    forces = pl.pallas_call(
        forces_kernel,
        out_shape=jax.ShapeDtypeStruct((16, targets), f32),
        in_specs=[pl.BlockSpec(memory_space=pltpu.VMEM)] * 6,
        out_specs=pl.BlockSpec(memory_space=pltpu.VMEM),
        scratch_shapes=[
            pltpu.VMEM((BLOCKS, 16, half), f32),
            pltpu.VMEM((16, targets), f32),
            pltpu.VMEM((3, 16, targets), f32),
            pltpu.VMEM((3, 96, targets), bf16),
            pltpu.VMEM((2, 3, CHUNK * half, targets), f32),
            pltpu.VMEM((3, 48, targets), f32),
            pltpu.VMEM((3, 32, targets), f32),
            pltpu.VMEM((16, targets), f32),
            pltpu.VMEM((16, targets), f32),
            pltpu.SemaphoreType.DMA((count,)),
            pltpu.SemaphoreType.DMA((count,)),
            pltpu.SemaphoreType.DMA((2,)),
        ],
        compiler_params=pltpu.CompilerParams(
            collective_id=0, has_side_effects=True, vmem_limit_bytes=48 * 2**20
        ),
    )(positions, velocities, accelerations, jerks, snaps, masses.reshape(1, targets))
    return correct(positions, velocities, accelerations, jerks, snaps, forces)


def solution(mesh):
    return jax.shard_map(
        shards,
        mesh=mesh,
        in_specs=(P(None, "wide"),) * 5 + (P("wide"),),
        out_specs=(P(None, "wide"),) * 6,
        check_vma=False,
    )
```

```python
import functools

import jax
import jax.numpy as jnp
from jax import lax
from jax.experimental import pallas as pl
from jax.experimental.pallas import tpu as pltpu
from jax.sharding import PartitionSpec as P

softening = 0.01
time_step = 0.0625

bf16 = jnp.bfloat16
f32 = jnp.float32
f8 = jnp.float8_e4m3fn
f8_wide = jnp.float8_e5m2
MESH = pl.DeviceIdType.MESH

CORES, NZ, NX, NY = 2, 8, 2, 4
BLOCKS = CORES * NZ * NX * NY
CHUNK = 2
PARTS = 2
STEP = CHUNK * PARTS
TILE = 256

Q_SCALE = 2.0**-4
P_SCALE = 2.0**-9.5
G_SCALE = 0.2 * 2.0**-15
W_BACK = 2.0**-6
C1_BACK = 2.0**-0.5
C2_BACK = 2.0**5
FINE_ROWS = ((0, 32), (32, 64), (64, 80))


def predict(positions, velocities, accelerations, jerks, snaps):
    pred_x = (
        positions
        + time_step * velocities
        + time_step * time_step / 2.0 * accelerations
        + time_step**3 / 6.0 * jerks
        + time_step**4 / 24.0 * snaps
    )
    pred_v = (
        velocities
        + time_step * accelerations
        + time_step * time_step / 2.0 * jerks
        + time_step**3 / 6.0 * snaps
    )
    pred_a = accelerations + time_step * jerks + time_step * time_step / 2.0 * snaps
    return (pred_x, pred_v, pred_a)


def correct(positions, velocities, accelerations, jerks, snaps, forces):
    new_acc = forces[0:3]
    new_jerk = forces[3:6]
    new_snap = forces[6:9]
    new_vel = (
        velocities
        + time_step / 2.0 * (new_acc + accelerations)
        - time_step * time_step / 10.0 * (new_jerk - jerks)
        + time_step**3 / 120.0 * (new_snap + snaps)
    )
    new_pos = (
        positions
        + time_step / 2.0 * (new_vel + velocities)
        - time_step * time_step / 10.0 * (new_acc - accelerations)
        + time_step**3 / 120.0 * (new_jerk + jerks)
    )
    first = new_acc - accelerations - time_step * jerks - time_step * time_step / 2.0 * snaps
    second = time_step * (new_jerk - jerks - time_step * snaps)
    third = time_step * time_step * (new_snap - snaps)
    crackle = 60.0 * first - 36.0 * second + 9.0 * third
    return (new_pos, new_vel, new_acc, new_jerk, new_snap, crackle)


def transfers():
    plan = []

    def put(step, to, src, dst, count=1):
        plan.append((step, to, src, dst, count))

    for to, dst in (
        ("core", 1), ("y+", 2), ("y-", 3), ("x", 4), ("y+ core", 5), ("z-", 16), ("z+", 32),
    ):
        put(-1, to, 0, dst)
    put(0, "y+", 2, 12)
    put(0, "x", 2, 8, 2)
    put(0, "core", 3, 6, 2)
    put(0, "z-", 2, 17, 3)
    put(0, "z+", 2, 33, 3)
    put(1, "x", 12, 13)
    put(1, "core", 8, 10, 2)
    put(1, "z-", 8, 20, 2)
    put(1, "z+", 8, 36, 2)
    put(2, "core", 12, 14, 2)
    put(2, "z-", 12, 22, 2)
    put(2, "z+", 12, 38, 2)
    put(4, "core", 16, 24, 8)
    put(4, "z-", 16, 48, 8)
    put(7, "core", 32, 40, 8)
    put(7, "z+", 32, 64, 8)
    put(8, "core", 48, 56, 8)
    put(8, "z-", 48, 80, 8)
    put(11, "core", 64, 72, 8)
    put(11, "z+", 64, 96, 8)
    put(12, "core", 80, 88, 8)
    put(12, "z-", 80, 112, 8)
    put(15, "core", 96, 104, 8)
    put(16, "core", 112, 120, 8)
    return plan


def waits(plan):
    due = []
    for _, _, _, dst, count in plan:
        use = max(-1, -((5 - dst) // STEP))
        for step, _, src, _, length in plan:
            if src < dst + count and dst < src + length:
                use = min(use, step)
        due.append(use)
    return due


def split3(value):
    high = value.astype(bf16)
    rest = value - high.astype(f32)
    middle = rest.astype(bf16)
    low = (rest - middle.astype(f32)).astype(bf16)
    return high, middle, low


def product(left, right, over_left):
    return lax.dot_general(
        left, right, (((over_left,), (0,)), ((), ())), preferred_element_type=f32
    )


def source_rows(block):
    high, middle, low = split3(block)
    return jnp.concatenate([high, high, high, middle, middle, low], axis=0)


def sum_rows(block):
    weighed = block * block[7:8]
    high, middle, low = [part.astype(f32) for part in split3(weighed)]
    none = jnp.zeros_like(weighed[0:8])
    fine = (
        jnp.concatenate([high, middle], axis=0).astype(bf16),
        jnp.concatenate([high[0:8], middle[0:8], low[0:8], none], axis=0).astype(bf16),
        jnp.concatenate([high[0:4], middle[0:4], low[0:4], none[0:4]], axis=0).astype(bf16),
    )
    first = weighed.astype(f8).astype(f32)
    second = weighed - first
    narrow = jnp.concatenate([first, second], axis=0).astype(f8)
    first = weighed[0:8].astype(f8_wide).astype(f32)
    second = (weighed[0:8] - first).astype(f8_wide).astype(f32)
    third = weighed[0:8] - first - second
    broad = jnp.concatenate([first, second, third, none], axis=0).astype(f8_wide)
    return fine, (narrow, narrow, broad)


def forces_kernel(
    pos_hbm, vel_hbm, acc_hbm, jerk_hbm, snap_hbm, mass_hbm, out_ref,
    pos_ref, vel_ref, acc_ref, jerk_ref, snap_ref, mass_ref, slots, own, feature, weights, pairs, total, total_low, part, other,
    load_sem, send_sem, recv_sem, narrow_sem,
):
    loads = [
        pltpu.make_async_copy(src, dst, load_sem.at[number])
        for number, (src, dst) in enumerate((
            (pos_hbm, pos_ref), (vel_hbm, vel_ref), (acc_hbm, acc_ref),
            (jerk_hbm, jerk_ref), (snap_hbm, snap_ref), (mass_hbm, mass_ref),
        ))
    ]
    for load in loads:
        load.start()
    wide, narrow = lax.axis_index("wide"), lax.axis_index("narrow")
    core, z = wide % CORES, (wide // CORES) % NZ
    x, y = (wide // (CORES * NZ)) % NX, wide // (CORES * NZ * NX)

    def index(y, x, z, core):
        return ((y * NX + x) * NZ + z) * CORES + core

    partner = {
        "core": {"wide": index(y, x, z, 1 - core)},
        "z+": {"wide": index(y, x, (z + 1) % NZ, core)},
        "z-": {"wide": index(y, x, (z + NZ - 1) % NZ, core)},
        "y+": {"wide": index((y + 1) % NY, x, z, core)},
        "y-": {"wide": index((y + NY - 1) % NY, x, z, core)},
        "x": {"wide": index(y, 1 - x, z, core)},
        "y+ core": {"wide": index((y + 1) % NY, x, z, 1 - core)},
        "narrow": {"narrow": 1 - narrow},
    }
    barrier = pltpu.get_barrier_semaphore()
    senders = dict(partner)
    senders["y+ core"] = {"wide": index((y + NY - 1) % NY, x, z, 1 - core)}
    for device in senders.values():
        pl.semaphore_signal(barrier, inc=1, device_id=device, device_id_type=MESH)
    for load in loads:
        load.wait()

    star_x, star_v, star_a = predict(
        pos_ref[...], vel_ref[...], acc_ref[...], jerk_ref[...], snap_ref[...]
    )
    targets = star_x.shape[1]
    half = targets // 2
    xx = jnp.sum(star_x * star_x, axis=0, keepdims=True)
    xv = jnp.sum(star_x * star_v, axis=0, keepdims=True)
    vv = jnp.sum(star_v * star_v, axis=0, keepdims=True) + jnp.sum(
        star_x * star_a, axis=0, keepdims=True
    )
    one = jnp.ones_like(xx)
    own[...] = jnp.zeros_like(own)
    for row, value in (
        (0, star_x), (3, one), (4, star_v), (7, mass_ref[...]), (8, star_a), (11, xx), (12, xv), (13, vv),
    ):
        own[row : row + value.shape[0], :] = value
    start = pl.multiple_of(narrow * half, half)
    slots[0] = own[:, pl.ds(start, half)]
    pl.semaphore_wait(barrier, len(partner))

    plan = transfers()
    due = waits(plan)

    def copy(number):
        _, to, src, dst, count = plan[number]
        return pltpu.make_async_remote_copy(
            src_ref=slots.at[pl.ds(src, count)],
            dst_ref=slots.at[pl.ds(dst, count)],
            send_sem=send_sem.at[number],
            recv_sem=recv_sem.at[number],
            device_id=partner[to],
            device_id_type=MESH,
        )

    def exchange(step):
        for number in range(len(plan)):
            if due[number] == step and plan[number][0] < step:
                copy(number).wait_recv()
        for number in range(len(plan)):
            if plan[number][0] == step:
                copy(number).start()
        for number in range(len(plan)):
            if due[number] == step and plan[number][0] >= step:
                copy(number).wait_recv()

    for number in range(len(plan)):
        if plan[number][0] == -1:
            copy(number).start()

    feature[...] = jnp.zeros_like(feature)
    for kind, rows in enumerate((
        ((0, -2.0 * Q_SCALE * star_x), (3, Q_SCALE * (xx + softening)), (11, Q_SCALE * one)),
        ((0, -P_SCALE * star_v), (3, P_SCALE * xv), (4, -P_SCALE * star_x), (12, P_SCALE * one)),
        (
            (0, -G_SCALE * star_a), (3, G_SCALE * vv), (4, -2.0 * G_SCALE * star_v),
            (8, -G_SCALE * star_x), (13, G_SCALE * one),
        ),
    )):
        for row, value in rows:
            feature[kind, row : row + value.shape[0], :] = value
        high, middle, low = split3(feature[kind])
        weights[kind] = jnp.concatenate([high, middle, low, high, middle, high], axis=0)

    total[...] = jnp.zeros_like(total)
    total_low[...] = jnp.zeros_like(total_low)

    def chunk_of(number):
        return jnp.concatenate([slots[number * CHUNK + u] for u in range(CHUNK)], axis=1)

    def forward(rows, parity, kind, tile):
        columns = slice(tile * TILE, (tile + 1) * TILE)
        pairs[parity, kind, :, columns] = product(rows, weights[kind, :, columns], 0)

    for number in range(len(plan)):
        if plan[number][0] == -1 and due[number] == -1:
            copy(number).wait_recv()
    rows = source_rows(chunk_of(0))
    for kind in range(3):
        for tile in range(targets // TILE):
            forward(rows, 0, kind, tile)

    steps = BLOCKS // STEP
    events = sorted(set([d for d in due if d >= 0] + [t[0] for t in plan if t[0] >= 0]))

    def branch(step, numbers):
        if len(numbers) <= 2:
            for number in numbers:
                pl.when(step == number)(functools.partial(exchange, number))
            return
        middle = len(numbers) // 2
        first, second = numbers[:middle], numbers[middle:]
        pl.when(step < second[0])(functools.partial(branch, step, first))
        pl.when(step >= second[0])(functools.partial(branch, step, second))

    def body(step, carry):
        branch(step, events)
        for parity in range(PARTS):
            chunk = step * PARTS + parity
            now, later = parity % 2, (parity + 1) % 2
            fine, coarse = sum_rows(chunk_of(chunk))
            ahead = source_rows(chunk_of(lax.min(chunk + 1, BLOCKS // CHUNK - 1)))
            work = [(kind, tile) for kind in range(3) for tile in range(targets // TILE)]
            units = [(b, tile) for b in range(CHUNK) for tile in range(targets // TILE)]
            done = 0
            for place, (b, tile) in enumerate(units):
                js = slice(b * half, (b + 1) * half)
                columns = slice(tile * TILE, (tile + 1) * TILE)
                q, p, g = [pairs[now, kind, js, columns] for kind in range(3)]
                root = lax.rsqrt(q)
                inverse = root * root
                w = inverse * root
                radial = p * inverse
                c1 = radial * w
                c2 = (w * inverse) * (p * radial - g)
                for kind, value in enumerate((w, c1, c2)):
                    high = value.astype(bf16)
                    low = (value - high.astype(f32)).astype(coarse[kind].dtype)
                    begin, end = FINE_ROWS[kind]
                    total[begin:end, columns] += product(fine[kind][:, js], high, 1)
                    total_low[kind, :, columns] += product(coarse[kind][:, js], low, 1)
                until = (place + 1) * len(work) // len(units)
                for kind, at in work[done:until]:
                    forward(ahead, later, kind, at)
                done = until
        return carry

    lax.fori_loop(0, steps, body, 0)

    sw = total[0:16] + total[16:32] + total_low[0, 0:16] + total_low[0, 16:32]
    s1 = total[32:40] + total[40:48] + total[48:56] + total_low[1, 0:8] + total_low[1, 16:24]
    s2 = (
        total[64:68] + total[68:72] + total[72:76]
        + total_low[2, 0:4] + total_low[2, 8:12] + total_low[2, 16:20]
    )
    share = 1.0 / (targets * BLOCKS)
    star_x, star_v, star_a = own[0:3, :], own[4:7, :], own[8:11, :]
    part[...] = jnp.zeros_like(part)
    part[0:3, :] = (W_BACK * share) * (sw[0:3] - star_x * sw[3:4])
    c1x = (C1_BACK * share) * (s1[0:3] - star_x * s1[3:4])
    part[3:6, :] = (W_BACK * share) * (sw[4:7] - star_v * sw[3:4]) - 3.0 * c1x
    part[6:9, :] = (
        (W_BACK * share) * (sw[8:11] - star_a * sw[3:4])
        - (6.0 * C1_BACK * share) * (s1[4:7] - star_v * s1[3:4])
        + (15.0 * C2_BACK * share) * (s2[0:3] - star_x * s2[3:4])
    )
    swap = pltpu.make_async_remote_copy(
        src_ref=part,
        dst_ref=other,
        send_sem=narrow_sem.at[0],
        recv_sem=narrow_sem.at[1],
        device_id=partner["narrow"],
        device_id_type=MESH,
    )
    swap.start()
    for number in range(len(plan)):
        copy(number).wait_send()
    swap.wait()
    out_ref[...] = part[...] + other[...]


def shards(positions, velocities, accelerations, jerks, snaps, masses):
    targets = positions.shape[1]
    half = targets // 2
    count = len(transfers())
    forces = pl.pallas_call(
        forces_kernel,
        out_shape=jax.ShapeDtypeStruct((16, targets), f32),
        in_specs=[pl.BlockSpec(memory_space=pltpu.HBM)] * 6,
        out_specs=pl.BlockSpec(memory_space=pltpu.VMEM),
        scratch_shapes=[pltpu.VMEM((3, targets), f32) for _ in range(5)]
        + [
            pltpu.VMEM((1, targets), f32),
            pltpu.VMEM((BLOCKS, 16, half), f32),
            pltpu.VMEM((16, targets), f32),
            pltpu.VMEM((3, 16, targets), f32),
            pltpu.VMEM((3, 96, targets), bf16),
            pltpu.VMEM((2, 3, CHUNK * half, targets), f32),
            pltpu.VMEM((80, targets), f32),
            pltpu.VMEM((3, 32, targets), f32),
            pltpu.VMEM((16, targets), f32),
            pltpu.VMEM((16, targets), f32),
            pltpu.SemaphoreType.DMA((6,)),
            pltpu.SemaphoreType.DMA((count,)),
            pltpu.SemaphoreType.DMA((count,)),
            pltpu.SemaphoreType.DMA((2,)),
        ],
        compiler_params=pltpu.CompilerParams(
            collective_id=0, has_side_effects=True, vmem_limit_bytes=60 * 2**20
        ),
    )(positions, velocities, accelerations, jerks, snaps, masses.reshape(1, targets))
    return correct(positions, velocities, accelerations, jerks, snaps, forces)


def solution(mesh):
    return jax.shard_map(
        shards,
        mesh=mesh,
        in_specs=(P(None, "wide"),) * 5 + (P("wide"),),
        out_specs=(P(None, "wide"),) * 6,
        check_vma=False,
    )
```

```python
import functools

import jax
import jax.numpy as jnp
from jax import lax
from jax.experimental import pallas as pl
from jax.experimental.pallas import tpu as pltpu
from jax.sharding import PartitionSpec as P

softening = 0.01
time_step = 0.0625

bf16 = jnp.bfloat16
f32 = jnp.float32
f8 = jnp.float8_e4m3fn
f8_wide = jnp.float8_e5m2
MESH = pl.DeviceIdType.MESH

CORES, NZ, NX, NY = 2, 8, 2, 4
BLOCKS = CORES * NZ * NX * NY
CHUNK = 2
PARTS = 2
STEP = CHUNK * PARTS
EARLY = 8
LATE_PARTS = 4
TILE = 256

Q_SCALE = 2.0**-4
P_SCALE = 2.0**-9.5
G_SCALE = 0.2 * 2.0**-15
W_BACK = 2.0**-6
C1_BACK = 2.0**-0.5
C2_BACK = 2.0**5
FINE_ROWS = ((0, 32), (32, 64), (64, 80))


def predict(positions, velocities, accelerations, jerks, snaps):
    pred_x = (
        positions
        + time_step * velocities
        + time_step * time_step / 2.0 * accelerations
        + time_step**3 / 6.0 * jerks
        + time_step**4 / 24.0 * snaps
    )
    pred_v = (
        velocities
        + time_step * accelerations
        + time_step * time_step / 2.0 * jerks
        + time_step**3 / 6.0 * snaps
    )
    pred_a = accelerations + time_step * jerks + time_step * time_step / 2.0 * snaps
    return (pred_x, pred_v, pred_a)


def correct(positions, velocities, accelerations, jerks, snaps, forces):
    new_acc = forces[0:3]
    new_jerk = forces[3:6]
    new_snap = forces[6:9]
    new_vel = (
        velocities
        + time_step / 2.0 * (new_acc + accelerations)
        - time_step * time_step / 10.0 * (new_jerk - jerks)
        + time_step**3 / 120.0 * (new_snap + snaps)
    )
    new_pos = (
        positions
        + time_step / 2.0 * (new_vel + velocities)
        - time_step * time_step / 10.0 * (new_acc - accelerations)
        + time_step**3 / 120.0 * (new_jerk + jerks)
    )
    first = new_acc - accelerations - time_step * jerks - time_step * time_step / 2.0 * snaps
    second = time_step * (new_jerk - jerks - time_step * snaps)
    third = time_step * time_step * (new_snap - snaps)
    crackle = 60.0 * first - 36.0 * second + 9.0 * third
    return (new_pos, new_vel, new_acc, new_jerk, new_snap, crackle)


def transfers():
    plan = []

    def put(step, to, src, dst, count=1):
        plan.append((step, to, src, dst, count))

    for to, dst in (("core", 1), ("y+", 2), ("y-", 3), ("x", 4), ("y+ core", 5)):
        put(-1, to, 0, dst)
    put(0, "y+", 2, 12)
    put(0, "x", 2, 8, 2)
    put(0, "core", 3, 6, 2)
    put(1, "x", 12, 13)
    put(1, "core", 8, 10, 2)
    for first, to, base in ((2, "z-", 16), (1, "z+", 32)):
        put(first, to, 0, base)
        put(first, to, 2, base + 1, 3)
        put(first, to, 8, base + 4, 2)
        put(2, to, 12, base + 6, 2)
    put(2, "core", 12, 14, 2)
    put(4, "core", 16, 24, 8)
    put(4, "z-", 16, 48, 8)
    put(7, "core", 32, 40, 8)
    put(7, "z+", 32, 64, 8)
    put(8, "core", 48, 56, 8)
    put(8, "z-", 48, 80, 8)
    put(12, "core", 64, 72, 8)
    put(12, "z+", 64, 96, 8)
    put(12, "core", 80, 88, 8)
    put(12, "z-", 80, 112, 8)
    put(16, "core", 96, 104, 8)
    put(16, "core", 112, 120, 8)
    return plan


def waits(plan):
    due = []
    for _, _, _, dst, count in plan:
        use = max(-1, -((5 - dst) // STEP))
        if use >= EARLY:
            use -= (use - EARLY) % (LATE_PARTS // PARTS)
        for step, _, src, _, length in plan:
            if src < dst + count and dst < src + length:
                use = min(use, step)
        due.append(use)
    return due


def split3(value):
    high = value.astype(bf16)
    rest = value - high.astype(f32)
    middle = rest.astype(bf16)
    low = (rest - middle.astype(f32)).astype(bf16)
    return high, middle, low


def product(left, right, over_left):
    return lax.dot_general(
        left, right, (((over_left,), (0,)), ((), ())), preferred_element_type=f32
    )


def source_rows(block):
    high, middle, low = split3(block)
    return jnp.concatenate([high, high, high, middle, middle, low], axis=0)


def sum_rows(block):
    weighed = block * block[7:8]
    high, middle, low = [part.astype(f32) for part in split3(weighed)]
    none = jnp.zeros_like(weighed[0:8])
    fine = (
        jnp.concatenate([high, middle], axis=0).astype(bf16),
        jnp.concatenate([high[0:8], middle[0:8], low[0:8], none], axis=0).astype(bf16),
        jnp.concatenate([high[0:4], middle[0:4], low[0:4], none[0:4]], axis=0).astype(bf16),
    )
    first = weighed.astype(f8).astype(f32)
    second = weighed - first
    narrow = jnp.concatenate([first, second], axis=0).astype(f8)
    first = weighed[0:8].astype(f8_wide).astype(f32)
    second = (weighed[0:8] - first).astype(f8_wide).astype(f32)
    third = weighed[0:8] - first - second
    broad = jnp.concatenate([first, second, third, none], axis=0).astype(f8_wide)
    return fine, (narrow, narrow, broad)


def forces_kernel(
    pos_hbm, vel_hbm, acc_hbm, jerk_hbm, snap_hbm, mass_hbm, out_ref,
    pos_ref, vel_ref, acc_ref, jerk_ref, snap_ref, mass_ref, slots, own, feature, weights, pairs, total, total_low, part, other,
    far_sem, load_sem, send_sem, recv_sem, narrow_sem,
):
    loads = [
        pltpu.make_async_copy(src, dst, load_sem.at[number])
        for number, (src, dst) in enumerate((
            (pos_hbm, pos_ref), (vel_hbm, vel_ref), (acc_hbm, acc_ref),
            (jerk_hbm, jerk_ref), (snap_hbm, snap_ref), (mass_hbm, mass_ref),
        ))
    ]
    for load in loads:
        load.start()
    wide, narrow = lax.axis_index("wide"), lax.axis_index("narrow")
    core, z = wide % CORES, (wide // CORES) % NZ
    x, y = (wide // (CORES * NZ)) % NX, wide // (CORES * NZ * NX)

    def index(y, x, z, core):
        return ((y * NX + x) * NZ + z) * CORES + core

    partner = {
        "core": {"wide": index(y, x, z, 1 - core)},
        "z+": {"wide": index(y, x, (z + 1) % NZ, core)},
        "z-": {"wide": index(y, x, (z + NZ - 1) % NZ, core)},
        "y+": {"wide": index((y + 1) % NY, x, z, core)},
        "y-": {"wide": index((y + NY - 1) % NY, x, z, core)},
        "x": {"wide": index(y, 1 - x, z, core)},
        "y+ core": {"wide": index((y + 1) % NY, x, z, 1 - core)},
        "narrow": {"narrow": 1 - narrow},
    }
    barrier = pltpu.get_barrier_semaphore()
    senders = dict(partner)
    senders["y+ core"] = {"wide": index((y + NY - 1) % NY, x, z, 1 - core)}
    for to, device in senders.items():
        if to != "z+":
            pl.semaphore_signal(barrier, inc=1, device_id=device, device_id_type=MESH)
    for load in loads:
        load.wait()

    star_x, star_v, star_a = predict(
        pos_ref[...], vel_ref[...], acc_ref[...], jerk_ref[...], snap_ref[...]
    )
    targets = star_x.shape[1]
    half = targets // 2
    xx = jnp.sum(star_x * star_x, axis=0, keepdims=True)
    xv = jnp.sum(star_x * star_v, axis=0, keepdims=True)
    vv = jnp.sum(star_v * star_v, axis=0, keepdims=True) + jnp.sum(
        star_x * star_a, axis=0, keepdims=True
    )
    one = jnp.ones_like(xx)
    own[...] = jnp.zeros_like(own)
    for row, value in (
        (0, star_x), (3, one), (4, star_v), (7, mass_ref[...]), (8, star_a), (11, xx), (12, xv), (13, vv),
    ):
        own[row : row + value.shape[0], :] = value
    start = pl.multiple_of(narrow * half, half)
    slots[0] = own[:, pl.ds(start, half)]
    pl.semaphore_wait(barrier, len(partner) - 1)
    pl.semaphore_signal(far_sem, inc=1, device_id=partner["z+"], device_id_type=MESH)

    plan = transfers()
    due = waits(plan)

    def copy(number):
        _, to, src, dst, count = plan[number]
        return pltpu.make_async_remote_copy(
            src_ref=slots.at[pl.ds(src, count)],
            dst_ref=slots.at[pl.ds(dst, count)],
            send_sem=send_sem.at[number],
            recv_sem=recv_sem.at[number],
            device_id=partner[to],
            device_id_type=MESH,
        )

    def exchange(step):
        for number in range(len(plan)):
            if due[number] == step and plan[number][0] < step:
                copy(number).wait_recv()
        if step == min(t[0] for t in plan if t[1] == "z-"):
            pl.semaphore_wait(far_sem, 1)
        for number in range(len(plan)):
            if plan[number][0] == step:
                copy(number).start()
        for number in range(len(plan)):
            if due[number] == step and plan[number][0] >= step:
                copy(number).wait_recv()

    for number in range(len(plan)):
        if plan[number][0] == -1:
            copy(number).start()

    feature[...] = jnp.zeros_like(feature)
    for kind, rows in enumerate((
        ((0, -2.0 * Q_SCALE * star_x), (3, Q_SCALE * (xx + softening)), (11, Q_SCALE * one)),
        ((0, -P_SCALE * star_v), (3, P_SCALE * xv), (4, -P_SCALE * star_x), (12, P_SCALE * one)),
        (
            (0, -G_SCALE * star_a), (3, G_SCALE * vv), (4, -2.0 * G_SCALE * star_v),
            (8, -G_SCALE * star_x), (13, G_SCALE * one),
        ),
    )):
        for row, value in rows:
            feature[kind, row : row + value.shape[0], :] = value
        high, middle, low = split3(feature[kind])
        weights[kind] = jnp.concatenate([high, middle, low, high, middle, high], axis=0)

    total[...] = jnp.zeros_like(total)
    total_low[...] = jnp.zeros_like(total_low)

    def chunk_of(number):
        return jnp.concatenate([slots[number * CHUNK + u] for u in range(CHUNK)], axis=1)

    def forward(rows, parity, kind, tile):
        columns = slice(tile * TILE, (tile + 1) * TILE)
        pairs[parity, kind, :, columns] = product(rows, weights[kind, :, columns], 0)

    for number in range(len(plan)):
        if plan[number][0] == -1 and due[number] == -1:
            copy(number).wait_recv()
    rows = source_rows(chunk_of(0))
    for kind in range(3):
        for tile in range(targets // TILE):
            forward(rows, 0, kind, tile)

    events = sorted(set([d for d in due if d >= 0] + [t[0] for t in plan if t[0] >= 0]))

    def branch(step, numbers):
        if len(numbers) <= 2:
            for number in numbers:
                pl.when(step == number)(functools.partial(exchange, number))
            return
        middle = len(numbers) // 2
        first, second = numbers[:middle], numbers[middle:]
        pl.when(step < second[0])(functools.partial(branch, step, first))
        pl.when(step >= second[0])(functools.partial(branch, step, second))

    def body(parts, numbers, step, carry):
        branch(step, numbers)
        for parity in range(parts):
            chunk = step * PARTS + parity
            now, later = parity % 2, (parity + 1) % 2
            fine, coarse = sum_rows(chunk_of(chunk))
            ahead = source_rows(chunk_of(lax.min(chunk + 1, BLOCKS // CHUNK - 1)))
            work = [(kind, tile) for tile in range(targets // TILE) for kind in range(3)]
            units = [(b, tile) for tile in range(targets // TILE) for b in range(CHUNK)]
            done = 0
            for place, (b, tile) in enumerate(units):
                js = slice(b * half, (b + 1) * half)
                columns = slice(tile * TILE, (tile + 1) * TILE)
                q, p, g = [pairs[now, kind, js, columns] for kind in range(3)]
                root = lax.rsqrt(q)
                inverse = pl.reciprocal(q, approx=True)
                w = inverse * root
                radial = p * inverse
                c1 = radial * w
                c2 = (w * inverse) * (p * radial - g)
                for kind, value in enumerate((w, c1, c2)):
                    high = value.astype(bf16)
                    low = (value - high.astype(f32)).astype(coarse[kind].dtype)
                    begin, end = FINE_ROWS[kind]
                    total[begin:end, columns] += product(fine[kind][:, js], high, 1)
                    total_low[kind, :, columns] += product(coarse[kind][:, js], low, 1)
                until = (place + 1) * len(work) // len(units)
                for kind, at in work[done:until]:
                    forward(ahead, later, kind, at)
                done = until
        return carry

    early = functools.partial(body, PARTS, [e for e in events if e < EARLY])
    lax.fori_loop(0, EARLY, early, 0)
    late = functools.partial(body, LATE_PARTS, [e for e in events if e >= EARLY])
    stride = LATE_PARTS // PARTS
    steps = (BLOCKS // STEP - EARLY) // stride
    lax.fori_loop(0, steps, lambda number, carry: late(EARLY + stride * number, carry), 0)

    sw = total[0:16] + total[16:32] + total_low[0, 0:16] + total_low[0, 16:32]
    s1 = total[32:40] + total[40:48] + total[48:56] + total_low[1, 0:8] + total_low[1, 16:24]
    s2 = (
        total[64:68] + total[68:72] + total[72:76]
        + total_low[2, 0:4] + total_low[2, 8:12] + total_low[2, 16:20]
    )
    share = 1.0 / (targets * BLOCKS)
    star_x, star_v, star_a = own[0:3, :], own[4:7, :], own[8:11, :]
    part[...] = jnp.zeros_like(part)
    part[0:3, :] = (W_BACK * share) * (sw[0:3] - star_x * sw[3:4])
    c1x = (C1_BACK * share) * (s1[0:3] - star_x * s1[3:4])
    part[3:6, :] = (W_BACK * share) * (sw[4:7] - star_v * sw[3:4]) - 3.0 * c1x
    part[6:9, :] = (
        (W_BACK * share) * (sw[8:11] - star_a * sw[3:4])
        - (6.0 * C1_BACK * share) * (s1[4:7] - star_v * s1[3:4])
        + (15.0 * C2_BACK * share) * (s2[0:3] - star_x * s2[3:4])
    )
    swap = pltpu.make_async_remote_copy(
        src_ref=part,
        dst_ref=other,
        send_sem=narrow_sem.at[0],
        recv_sem=narrow_sem.at[1],
        device_id=partner["narrow"],
        device_id_type=MESH,
    )
    swap.start()
    for number in range(len(plan)):
        copy(number).wait_send()
    swap.wait()
    out_ref[...] = part[...] + other[...]


def shards(positions, velocities, accelerations, jerks, snaps, masses):
    targets = positions.shape[1]
    half = targets // 2
    count = len(transfers())
    forces = pl.pallas_call(
        forces_kernel,
        out_shape=jax.ShapeDtypeStruct((16, targets), f32),
        in_specs=[pl.BlockSpec(memory_space=pltpu.HBM)] * 6,
        out_specs=pl.BlockSpec(memory_space=pltpu.VMEM),
        scratch_shapes=[pltpu.VMEM((3, targets), f32) for _ in range(5)]
        + [
            pltpu.VMEM((1, targets), f32),
            pltpu.VMEM((BLOCKS, 16, half), f32),
            pltpu.VMEM((16, targets), f32),
            pltpu.VMEM((3, 16, targets), f32),
            pltpu.VMEM((3, 96, targets), bf16),
            pltpu.VMEM((2, 3, CHUNK * half, targets), f32),
            pltpu.VMEM((80, targets), f32),
            pltpu.VMEM((3, 32, targets), f32),
            pltpu.VMEM((16, targets), f32),
            pltpu.VMEM((16, targets), f32),
            pltpu.SemaphoreType.REGULAR,
            pltpu.SemaphoreType.DMA((6,)),
            pltpu.SemaphoreType.DMA((count,)),
            pltpu.SemaphoreType.DMA((count,)),
            pltpu.SemaphoreType.DMA((2,)),
        ],
        compiler_params=pltpu.CompilerParams(
            collective_id=0, has_side_effects=True, vmem_limit_bytes=60 * 2**20
        ),
    )(positions, velocities, accelerations, jerks, snaps, masses.reshape(1, targets))
    return correct(positions, velocities, accelerations, jerks, snaps, forces)


def solution(mesh):
    return jax.shard_map(
        shards,
        mesh=mesh,
        in_specs=(P(None, "wide"),) * 5 + (P("wide"),),
        out_specs=(P(None, "wide"),) * 6,
        check_vma=False,
    )
```

```python
import functools

import jax
import jax.numpy as jnp
from jax import lax
from jax.experimental import pallas as pl
from jax.experimental.pallas import tpu as pltpu
from jax.sharding import PartitionSpec as P

softening = 0.01
time_step = 0.0625

bf16 = jnp.bfloat16
f32 = jnp.float32
f8 = jnp.float8_e4m3fn
f8_wide = jnp.float8_e5m2
MESH = pl.DeviceIdType.MESH

CORES, NZ, NX, NY = 2, 8, 2, 4
BLOCKS = CORES * NZ * NX * NY
CHUNK = 2
PARTS = 2
STEP = CHUNK * PARTS
EARLY = 8
LATE_PARTS = 8
FIRST_Z = 1
TILE = 256

Q_SCALE = 2.0**-4
P_SCALE = 2.0**-9.5
G_SCALE = 0.2 * 2.0**-15
W_BACK = 2.0**-6
C1_BACK = 2.0**-0.5
C2_BACK = 2.0**5
FINE_ROWS = ((0, 32), (32, 64), (64, 80))


def predict(positions, velocities, accelerations, jerks, snaps):
    pred_x = (
        positions
        + time_step * velocities
        + time_step * time_step / 2.0 * accelerations
        + time_step**3 / 6.0 * jerks
        + time_step**4 / 24.0 * snaps
    )
    pred_v = (
        velocities
        + time_step * accelerations
        + time_step * time_step / 2.0 * jerks
        + time_step**3 / 6.0 * snaps
    )
    pred_a = accelerations + time_step * jerks + time_step * time_step / 2.0 * snaps
    return (pred_x, pred_v, pred_a)


def correct(positions, velocities, accelerations, jerks, snaps, forces):
    new_acc = forces[0:3]
    new_jerk = forces[3:6]
    new_snap = forces[6:9]
    new_vel = (
        velocities
        + time_step / 2.0 * (new_acc + accelerations)
        - time_step * time_step / 10.0 * (new_jerk - jerks)
        + time_step**3 / 120.0 * (new_snap + snaps)
    )
    new_pos = (
        positions
        + time_step / 2.0 * (new_vel + velocities)
        - time_step * time_step / 10.0 * (new_acc - accelerations)
        + time_step**3 / 120.0 * (new_jerk + jerks)
    )
    first = new_acc - accelerations - time_step * jerks - time_step * time_step / 2.0 * snaps
    second = time_step * (new_jerk - jerks - time_step * snaps)
    third = time_step * time_step * (new_snap - snaps)
    crackle = 60.0 * first - 36.0 * second + 9.0 * third
    return (new_pos, new_vel, new_acc, new_jerk, new_snap, crackle)


def transfers():
    plan = []

    def put(step, to, src, dst, count=1):
        plan.append((step, to, src, dst, count))

    for to, dst in (("core", 1), ("y+", 2), ("y-", 3), ("x", 4), ("y+ core", 5)):
        put(-1, to, 0, dst)
    put(0, "y+", 2, 12)
    put(0, "x", 2, 8, 2)
    put(0, "core", 3, 6, 2)
    put(1, "x", 12, 13)
    put(1, "core", 8, 10, 2)
    for to, base in (("z-", 16), ("z+", 32)):
        put(FIRST_Z, to, 0, base)
        put(FIRST_Z, to, 2, base + 1, 3)
        put(FIRST_Z, to, 8, base + 4, 2)
        put(FIRST_Z + 1, to, 12, base + 6, 2)
    put(2, "core", 12, 14, 2)
    put(4, "core", 16, 24, 8)
    put(4, "z-", 16, 48, 8)
    put(7, "core", 32, 40, 8)
    put(7, "z+", 32, 64, 8)
    put(8, "core", 48, 56, 8)
    put(8, "z-", 48, 80, 8)
    put(12, "core", 64, 72, 8)
    put(12, "z+", 64, 96, 8)
    put(12, "core", 80, 88, 8)
    put(12, "z-", 80, 112, 8)
    put(16, "core", 96, 104, 8)
    put(16, "core", 112, 120, 8)
    return plan


def waits(plan):
    due = []
    for _, _, _, dst, count in plan:
        use = max(-1, -((5 - dst) // STEP))
        if use >= EARLY:
            use -= (use - EARLY) % (LATE_PARTS // PARTS)
        for step, _, src, _, length in plan:
            if src < dst + count and dst < src + length:
                use = min(use, step)
        due.append(use)
    return due


def split3(value):
    high = value.astype(bf16)
    rest = value - high.astype(f32)
    middle = rest.astype(bf16)
    low = (rest - middle.astype(f32)).astype(bf16)
    return high, middle, low


def product(left, right, over_left):
    return lax.dot_general(
        left, right, (((over_left,), (0,)), ((), ())), preferred_element_type=f32
    )


def source_rows(block):
    high, middle, low = split3(block)
    return jnp.concatenate([high, high, high, middle, middle, low], axis=0)


def sum_rows(block):
    weighed = block * block[7:8]
    high, middle, low = [part.astype(f32) for part in split3(weighed)]
    none = jnp.zeros_like(weighed[0:8])
    fine = (
        jnp.concatenate([high, middle], axis=0).astype(bf16),
        jnp.concatenate([high[0:8], middle[0:8], low[0:8], none], axis=0).astype(bf16),
        jnp.concatenate([high[0:4], middle[0:4], low[0:4], none[0:4]], axis=0).astype(bf16),
    )
    first = weighed.astype(f8).astype(f32)
    second = weighed - first
    narrow = jnp.concatenate([first, second], axis=0).astype(f8)
    first = weighed[0:8].astype(f8_wide).astype(f32)
    second = (weighed[0:8] - first).astype(f8_wide).astype(f32)
    third = weighed[0:8] - first - second
    broad = jnp.concatenate([first, second, third, none], axis=0).astype(f8_wide)
    return fine, (narrow, narrow, broad)


def forces_kernel(
    pos_hbm, vel_hbm, acc_hbm, jerk_hbm, snap_hbm, mass_hbm, out_ref,
    pos_ref, vel_ref, acc_ref, jerk_ref, snap_ref, mass_ref, slots, own, feature, weights, pairs, total, total_low, part, other,
    far_sem, load_sem, send_sem, recv_sem, narrow_sem,
):
    loads = [
        pltpu.make_async_copy(src, dst, load_sem.at[number])
        for number, (src, dst) in enumerate((
            (pos_hbm, pos_ref), (vel_hbm, vel_ref), (acc_hbm, acc_ref),
            (jerk_hbm, jerk_ref), (snap_hbm, snap_ref), (mass_hbm, mass_ref),
        ))
    ]
    for load in loads:
        load.start()
    wide, narrow = lax.axis_index("wide"), lax.axis_index("narrow")
    core, z = wide % CORES, (wide // CORES) % NZ
    x, y = (wide // (CORES * NZ)) % NX, wide // (CORES * NZ * NX)

    def index(y, x, z, core):
        return ((y * NX + x) * NZ + z) * CORES + core

    partner = {
        "core": {"wide": index(y, x, z, 1 - core)},
        "z+": {"wide": index(y, x, (z + 1) % NZ, core)},
        "z-": {"wide": index(y, x, (z + NZ - 1) % NZ, core)},
        "y+": {"wide": index((y + 1) % NY, x, z, core)},
        "y-": {"wide": index((y + NY - 1) % NY, x, z, core)},
        "x": {"wide": index(y, 1 - x, z, core)},
        "y+ core": {"wide": index((y + 1) % NY, x, z, 1 - core)},
        "narrow": {"narrow": 1 - narrow},
    }
    barrier = pltpu.get_barrier_semaphore()
    senders = dict(partner)
    senders["y+ core"] = {"wide": index((y + NY - 1) % NY, x, z, 1 - core)}
    lowest, highest = z == 0, z == NZ - 1
    for to, device in senders.items():
        if to not in ("z+", "z-"):
            pl.semaphore_signal(barrier, inc=1, device_id=device, device_id_type=MESH)

    @pl.when(jnp.logical_not(highest))
    def _():
        pl.semaphore_signal(barrier, inc=1, device_id=partner["z+"], device_id_type=MESH)

    @pl.when(lowest)
    def _():
        pl.semaphore_signal(barrier, inc=1, device_id=partner["z-"], device_id_type=MESH)
    for load in loads:
        load.wait()

    star_x, star_v, star_a = predict(
        pos_ref[...], vel_ref[...], acc_ref[...], jerk_ref[...], snap_ref[...]
    )
    targets = star_x.shape[1]
    half = targets // 2
    xx = jnp.sum(star_x * star_x, axis=0, keepdims=True)
    xv = jnp.sum(star_x * star_v, axis=0, keepdims=True)
    vv = jnp.sum(star_v * star_v, axis=0, keepdims=True) + jnp.sum(
        star_x * star_a, axis=0, keepdims=True
    )
    one = jnp.ones_like(xx)
    own[...] = jnp.zeros_like(own)
    for row, value in (
        (0, star_x), (3, one), (4, star_v), (7, mass_ref[...]), (8, star_a), (11, xx), (12, xv), (13, vv),
    ):
        own[row : row + value.shape[0], :] = value
    start = pl.multiple_of(narrow * half, half)
    slots[0] = own[:, pl.ds(start, half)]
    pl.semaphore_wait(barrier, len(partner) - 2 + lax.min(z, 1) + z // (NZ - 1))

    @pl.when(jnp.logical_not(lowest))
    def _():
        pl.semaphore_signal(far_sem.at[0], inc=1, device_id=partner["z-"], device_id_type=MESH)

    @pl.when(highest)
    def _():
        pl.semaphore_signal(far_sem.at[1], inc=1, device_id=partner["z+"], device_id_type=MESH)

    plan = transfers()
    due = waits(plan)

    def copy(number):
        _, to, src, dst, count = plan[number]
        return pltpu.make_async_remote_copy(
            src_ref=slots.at[pl.ds(src, count)],
            dst_ref=slots.at[pl.ds(dst, count)],
            send_sem=send_sem.at[number],
            recv_sem=recv_sem.at[number],
            device_id=partner[to],
            device_id_type=MESH,
        )

    def exchange(step):
        for number in range(len(plan)):
            if due[number] == step and plan[number][0] < step:
                copy(number).wait_recv()
        down = [n for n in range(len(plan)) if plan[n][:2] == (FIRST_Z, "z-")]
        if step == FIRST_Z:

            @pl.when(jnp.logical_not(highest))
            def _():
                pl.semaphore_wait(far_sem.at[0], 1)

            @pl.when(jnp.logical_not(lowest))
            def _():
                for number in down:
                    copy(number).start()

        if step == FIRST_Z + 1:

            @pl.when(lowest)
            def _():
                pl.semaphore_wait(far_sem.at[1], 1)
                for number in down:
                    copy(number).start()

        for number in range(len(plan)):
            if plan[number][0] == step and number not in down:
                copy(number).start()
        for number in range(len(plan)):
            if due[number] == step and plan[number][0] >= step:
                copy(number).wait_recv()

    for number in range(len(plan)):
        if plan[number][0] == -1:
            copy(number).start()

    feature[...] = jnp.zeros_like(feature)
    for kind, rows in enumerate((
        ((0, -2.0 * Q_SCALE * star_x), (3, Q_SCALE * (xx + softening)), (11, Q_SCALE * one)),
        ((0, -P_SCALE * star_v), (3, P_SCALE * xv), (4, -P_SCALE * star_x), (12, P_SCALE * one)),
        (
            (0, -G_SCALE * star_a), (3, G_SCALE * vv), (4, -2.0 * G_SCALE * star_v),
            (8, -G_SCALE * star_x), (13, G_SCALE * one),
        ),
    )):
        for row, value in rows:
            feature[kind, row : row + value.shape[0], :] = value
        high, middle, low = split3(feature[kind])
        weights[kind] = jnp.concatenate([high, middle, low, high, middle, high], axis=0)

    total[...] = jnp.zeros_like(total)
    total_low[...] = jnp.zeros_like(total_low)

    def chunk_of(number):
        return jnp.concatenate([slots[number * CHUNK + u] for u in range(CHUNK)], axis=1)

    def forward(rows, parity, kind, tile):
        columns = slice(tile * TILE, (tile + 1) * TILE)
        pairs[parity, kind, :, columns] = product(rows, weights[kind, :, columns], 0)

    for number in range(len(plan)):
        if plan[number][0] == -1 and due[number] == -1:
            copy(number).wait_recv()
    rows = source_rows(chunk_of(0))
    for kind in range(3):
        for tile in range(targets // TILE):
            forward(rows, 0, kind, tile)

    events = sorted(set([d for d in due if d >= 0] + [t[0] for t in plan if t[0] >= 0]))

    def branch(step, numbers):
        if len(numbers) <= 2:
            for number in numbers:
                pl.when(step == number)(functools.partial(exchange, number))
            return
        middle = len(numbers) // 2
        first, second = numbers[:middle], numbers[middle:]
        pl.when(step < second[0])(functools.partial(branch, step, first))
        pl.when(step >= second[0])(functools.partial(branch, step, second))

    def body(parts, numbers, step, carry):
        branch(step, numbers)
        for parity in range(parts):
            chunk = step * PARTS + parity
            now, later = parity % 2, (parity + 1) % 2
            fine, coarse = sum_rows(chunk_of(chunk))
            ahead = source_rows(chunk_of(lax.min(chunk + 1, BLOCKS // CHUNK - 1)))
            work = [(kind, tile) for tile in range(targets // TILE) for kind in range(3)]
            units = [(b, tile) for tile in range(targets // TILE) for b in range(CHUNK)]
            done = 0
            for place, (b, tile) in enumerate(units):
                js = slice(b * half, (b + 1) * half)
                columns = slice(tile * TILE, (tile + 1) * TILE)
                q, p, g = [pairs[now, kind, js, columns] for kind in range(3)]
                root = lax.rsqrt(q)
                inverse = pl.reciprocal(q, approx=True)
                w = inverse * root
                radial = p * inverse
                c1 = radial * w
                c2 = (w * inverse) * (p * radial - g)
                for kind, value in enumerate((w, c1, c2)):
                    high = value.astype(bf16)
                    low = (value - high.astype(f32)).astype(coarse[kind].dtype)
                    begin, end = FINE_ROWS[kind]
                    total[begin:end, columns] += product(fine[kind][:, js], high, 1)
                    total_low[kind, :, columns] += product(coarse[kind][:, js], low, 1)
                until = (place + 1) * len(work) // len(units)
                for kind, at in work[done:until]:
                    forward(ahead, later, kind, at)
                done = until
        return carry

    early = functools.partial(body, PARTS, [e for e in events if e < EARLY])
    lax.fori_loop(0, EARLY, early, 0)
    late = functools.partial(body, LATE_PARTS, [e for e in events if e >= EARLY])
    stride = LATE_PARTS // PARTS
    steps = (BLOCKS // STEP - EARLY) // stride
    lax.fori_loop(0, steps, lambda number, carry: late(EARLY + stride * number, carry), 0)

    sw = total[0:16] + total[16:32] + total_low[0, 0:16] + total_low[0, 16:32]
    s1 = total[32:40] + total[40:48] + total[48:56] + total_low[1, 0:8] + total_low[1, 16:24]
    s2 = (
        total[64:68] + total[68:72] + total[72:76]
        + total_low[2, 0:4] + total_low[2, 8:12] + total_low[2, 16:20]
    )
    share = 1.0 / (targets * BLOCKS)
    star_x, star_v, star_a = own[0:3, :], own[4:7, :], own[8:11, :]
    part[...] = jnp.zeros_like(part)
    part[0:3, :] = (W_BACK * share) * (sw[0:3] - star_x * sw[3:4])
    c1x = (C1_BACK * share) * (s1[0:3] - star_x * s1[3:4])
    part[3:6, :] = (W_BACK * share) * (sw[4:7] - star_v * sw[3:4]) - 3.0 * c1x
    part[6:9, :] = (
        (W_BACK * share) * (sw[8:11] - star_a * sw[3:4])
        - (6.0 * C1_BACK * share) * (s1[4:7] - star_v * s1[3:4])
        + (15.0 * C2_BACK * share) * (s2[0:3] - star_x * s2[3:4])
    )
    swap = pltpu.make_async_remote_copy(
        src_ref=part,
        dst_ref=other,
        send_sem=narrow_sem.at[0],
        recv_sem=narrow_sem.at[1],
        device_id=partner["narrow"],
        device_id_type=MESH,
    )
    swap.start()
    for number in range(len(plan)):
        copy(number).wait_send()
    swap.wait()
    out_ref[...] = part[...] + other[...]


def shards(positions, velocities, accelerations, jerks, snaps, masses):
    targets = positions.shape[1]
    half = targets // 2
    count = len(transfers())
    forces = pl.pallas_call(
        forces_kernel,
        out_shape=jax.ShapeDtypeStruct((16, targets), f32),
        in_specs=[pl.BlockSpec(memory_space=pltpu.HBM)] * 6,
        out_specs=pl.BlockSpec(memory_space=pltpu.VMEM),
        scratch_shapes=[pltpu.VMEM((3, targets), f32) for _ in range(5)]
        + [
            pltpu.VMEM((1, targets), f32),
            pltpu.VMEM((BLOCKS, 16, half), f32),
            pltpu.VMEM((16, targets), f32),
            pltpu.VMEM((3, 16, targets), f32),
            pltpu.VMEM((3, 96, targets), bf16),
            pltpu.VMEM((2, 3, CHUNK * half, targets), f32),
            pltpu.VMEM((80, targets), f32),
            pltpu.VMEM((3, 32, targets), f32),
            pltpu.VMEM((16, targets), f32),
            pltpu.VMEM((16, targets), f32),
            pltpu.SemaphoreType.REGULAR((2,)),
            pltpu.SemaphoreType.DMA((6,)),
            pltpu.SemaphoreType.DMA((count,)),
            pltpu.SemaphoreType.DMA((count,)),
            pltpu.SemaphoreType.DMA((2,)),
        ],
        compiler_params=pltpu.CompilerParams(
            collective_id=0, has_side_effects=True, vmem_limit_bytes=60 * 2**20
        ),
    )(positions, velocities, accelerations, jerks, snaps, masses.reshape(1, targets))
    return correct(positions, velocities, accelerations, jerks, snaps, forces)


def solution(mesh):
    return jax.shard_map(
        shards,
        mesh=mesh,
        in_specs=(P(None, "wide"),) * 5 + (P("wide"),),
        out_specs=(P(None, "wide"),) * 6,
        check_vma=False,
    )
```

```python
import functools

import jax
import jax.numpy as jnp
from jax import lax
from jax.experimental import pallas as pl
from jax.experimental.pallas import tpu as pltpu
from jax.sharding import PartitionSpec as P

softening = 0.01
time_step = 0.0625

bf16 = jnp.bfloat16
f32 = jnp.float32
f8 = jnp.float8_e4m3fn
f8_wide = jnp.float8_e5m2
MESH = pl.DeviceIdType.MESH

CORES, NZ, NX, NY = 2, 8, 2, 4
BLOCKS = CORES * NZ * NX * NY
CHUNK = 2
PARTS = 2
STEP = CHUNK * PARTS
EARLY = 8
LATE_PARTS = 8
FIRST_Z = 1
TILE = 256

Q_SCALE = 2.0**-4
P_SCALE = 2.0**-9.5
G_SCALE = 0.2 * 2.0**-15
W_BACK = 2.0**-6
C1_BACK = 2.0**-0.5
C2_BACK = 2.0**5
FINE_ROWS = ((0, 32), (32, 64), (64, 80))


def predict(positions, velocities, accelerations, jerks, snaps):
    pred_x = (
        positions
        + time_step * velocities
        + time_step * time_step / 2.0 * accelerations
        + time_step**3 / 6.0 * jerks
        + time_step**4 / 24.0 * snaps
    )
    pred_v = (
        velocities
        + time_step * accelerations
        + time_step * time_step / 2.0 * jerks
        + time_step**3 / 6.0 * snaps
    )
    pred_a = accelerations + time_step * jerks + time_step * time_step / 2.0 * snaps
    return (pred_x, pred_v, pred_a)


def correct(positions, velocities, accelerations, jerks, snaps, forces):
    new_acc = forces[0:3]
    new_jerk = forces[3:6]
    new_snap = forces[6:9]
    new_vel = (
        velocities
        + time_step / 2.0 * (new_acc + accelerations)
        - time_step * time_step / 10.0 * (new_jerk - jerks)
        + time_step**3 / 120.0 * (new_snap + snaps)
    )
    new_pos = (
        positions
        + time_step / 2.0 * (new_vel + velocities)
        - time_step * time_step / 10.0 * (new_acc - accelerations)
        + time_step**3 / 120.0 * (new_jerk + jerks)
    )
    first = new_acc - accelerations - time_step * jerks - time_step * time_step / 2.0 * snaps
    second = time_step * (new_jerk - jerks - time_step * snaps)
    third = time_step * time_step * (new_snap - snaps)
    crackle = 60.0 * first - 36.0 * second + 9.0 * third
    return (new_pos, new_vel, new_acc, new_jerk, new_snap, crackle)


def transfers():
    plan = []

    def put(step, to, src, dst, count=1):
        plan.append((step, to, src, dst, count))

    for to, dst in (("core", 1), ("y+", 2), ("y-", 3), ("x", 4), ("y+ core", 5)):
        put(-1, to, 0, dst)
    put(0, "y+", 2, 12)
    put(0, "x", 2, 8, 2)
    put(0, "core", 3, 6, 2)
    put(1, "x", 12, 13)
    put(1, "core", 8, 10, 2)
    for to, base in (("z-", 16), ("z+", 32)):
        put(FIRST_Z, to, 0, base)
        put(FIRST_Z, to, 2, base + 1, 3)
        put(FIRST_Z, to, 8, base + 4, 2)
        put(FIRST_Z + 1, to, 12, base + 6, 2)
    put(2, "core", 12, 14, 2)
    put(4, "core", 16, 24, 8)
    put(4, "z-", 16, 48, 8)
    put(7, "core", 32, 40, 8)
    put(7, "z+", 32, 64, 8)
    put(8, "core", 48, 56, 8)
    put(8, "z-", 48, 80, 8)
    put(12, "core", 64, 72, 8)
    put(12, "z+", 64, 96, 8)
    put(12, "core", 80, 88, 8)
    put(12, "z-", 80, 112, 8)
    put(16, "core", 96, 104, 8)
    put(16, "core", 112, 120, 8)
    return plan


def waits(plan):
    due = []
    for _, _, _, dst, count in plan:
        use = max(-1, -((5 - dst) // STEP))
        if use >= EARLY:
            use -= (use - EARLY) % (LATE_PARTS // PARTS)
        for step, _, src, _, length in plan:
            if src < dst + count and dst < src + length:
                use = min(use, step)
        due.append(use)
    return due


def split3(value):
    high = value.astype(bf16)
    rest = value - high.astype(f32)
    middle = rest.astype(bf16)
    low = (rest - middle.astype(f32)).astype(bf16)
    return high, middle, low


def product(left, right, over_left):
    return lax.dot_general(
        left, right, (((over_left,), (0,)), ((), ())), preferred_element_type=f32
    )


def source_rows(block):
    high, middle, low = split3(block)
    return jnp.concatenate([high, high, high, middle, middle, low], axis=0)


def sum_rows(block):
    weighed = block * block[7:8]
    high, middle, low = [part.astype(f32) for part in split3(weighed)]
    none = jnp.zeros_like(weighed[0:8])
    fine = (
        jnp.concatenate([high, middle], axis=0).astype(bf16),
        jnp.concatenate([high[0:8], middle[0:8], low[0:8], none], axis=0).astype(bf16),
        jnp.concatenate([high[0:4], middle[0:4], low[0:4], none[0:4]], axis=0).astype(bf16),
    )
    first = weighed.astype(f8).astype(f32)
    second = weighed - first
    narrow = jnp.concatenate([first, second], axis=0).astype(f8)
    first = weighed[0:8].astype(f8_wide).astype(f32)
    second = (weighed[0:8] - first).astype(f8_wide).astype(f32)
    third = weighed[0:8] - first - second
    broad = jnp.concatenate([first, second, third, none], axis=0).astype(f8_wide)
    return fine, (narrow, narrow, broad)


def forces_kernel(
    pos_hbm, vel_hbm, acc_hbm, jerk_hbm, snap_hbm, mass_hbm, out_ref,
    pos_ref, vel_ref, acc_ref, jerk_ref, snap_ref, mass_ref, slots, own, feature, weights, pairs, total, total_low, part, other,
    far_sem, load_sem, send_sem, recv_sem, narrow_sem,
):
    loads = [
        pltpu.make_async_copy(src, dst, load_sem.at[number])
        for number, (src, dst) in enumerate((
            (pos_hbm, pos_ref), (vel_hbm, vel_ref), (acc_hbm, acc_ref),
            (jerk_hbm, jerk_ref), (snap_hbm, snap_ref), (mass_hbm, mass_ref),
        ))
    ]
    for load in loads:
        load.start()
    wide, narrow = lax.axis_index("wide"), lax.axis_index("narrow")
    core, z = wide % CORES, (wide // CORES) % NZ
    x, y = (wide // (CORES * NZ)) % NX, wide // (CORES * NZ * NX)

    def index(y, x, z, core):
        return ((y * NX + x) * NZ + z) * CORES + core

    partner = {
        "core": {"wide": index(y, x, z, 1 - core)},
        "z+": {"wide": index(y, x, (z + 1) % NZ, core)},
        "z-": {"wide": index(y, x, (z + NZ - 1) % NZ, core)},
        "y+": {"wide": index((y + 1) % NY, x, z, core)},
        "y-": {"wide": index((y + NY - 1) % NY, x, z, core)},
        "x": {"wide": index(y, 1 - x, z, core)},
        "y+ core": {"wide": index((y + 1) % NY, x, z, 1 - core)},
        "narrow": {"narrow": 1 - narrow},
    }
    barrier = pltpu.get_barrier_semaphore()
    senders = dict(partner)
    senders["y+ core"] = {"wide": index((y + NY - 1) % NY, x, z, 1 - core)}
    lowest, highest = z == 0, z == NZ - 1
    for to, device in senders.items():
        if to not in ("z+", "z-"):
            pl.semaphore_signal(barrier, inc=1, device_id=device, device_id_type=MESH)

    @pl.when(jnp.logical_not(highest))
    def _():
        pl.semaphore_signal(barrier, inc=1, device_id=partner["z+"], device_id_type=MESH)

    @pl.when(lowest)
    def _():
        pl.semaphore_signal(barrier, inc=1, device_id=partner["z-"], device_id_type=MESH)
    for load in loads:
        load.wait()

    star_x, star_v, star_a = predict(
        pos_ref[...], vel_ref[...], acc_ref[...], jerk_ref[...], snap_ref[...]
    )
    targets = star_x.shape[1]
    half = targets // 2
    xx = jnp.sum(star_x * star_x, axis=0, keepdims=True)
    xv = jnp.sum(star_x * star_v, axis=0, keepdims=True)
    vv = jnp.sum(star_v * star_v, axis=0, keepdims=True) + jnp.sum(
        star_x * star_a, axis=0, keepdims=True
    )
    one = jnp.ones_like(xx)
    own[...] = jnp.zeros_like(own)
    for row, value in (
        (0, star_x), (3, one), (4, star_v), (7, mass_ref[...]), (8, star_a), (11, xx), (12, xv), (13, vv),
    ):
        own[row : row + value.shape[0], :] = value
    start = pl.multiple_of(narrow * half, half)
    slots[0] = own[:, pl.ds(start, half)]
    pl.semaphore_wait(barrier, len(partner) - 2 + lax.min(z, 1) + z // (NZ - 1))

    @pl.when(jnp.logical_not(lowest))
    def _():
        pl.semaphore_signal(far_sem.at[0], inc=1, device_id=partner["z-"], device_id_type=MESH)

    @pl.when(highest)
    def _():
        pl.semaphore_signal(far_sem.at[1], inc=1, device_id=partner["z+"], device_id_type=MESH)

    plan = transfers()
    due = waits(plan)

    def copy(number):
        _, to, src, dst, count = plan[number]
        return pltpu.make_async_remote_copy(
            src_ref=slots.at[pl.ds(src, count)],
            dst_ref=slots.at[pl.ds(dst, count)],
            send_sem=send_sem.at[number],
            recv_sem=recv_sem.at[number],
            device_id=partner[to],
            device_id_type=MESH,
        )

    def exchange(step):
        for number in range(len(plan)):
            if due[number] == step and plan[number][0] < step:
                copy(number).wait_recv()
        down = [n for n in range(len(plan)) if plan[n][:2] == (FIRST_Z, "z-")]
        if step == FIRST_Z:

            @pl.when(jnp.logical_not(highest))
            def _():
                pl.semaphore_wait(far_sem.at[0], 1)

            @pl.when(jnp.logical_not(lowest))
            def _():
                for number in down:
                    copy(number).start()

        if step == FIRST_Z + 1:

            @pl.when(lowest)
            def _():
                pl.semaphore_wait(far_sem.at[1], 1)
                for number in down:
                    copy(number).start()

        for number in range(len(plan)):
            if plan[number][0] == step and number not in down:
                copy(number).start()
        for number in range(len(plan)):
            if due[number] == step and plan[number][0] >= step:
                copy(number).wait_recv()

    for number in range(len(plan)):
        if plan[number][0] == -1:
            copy(number).start()

    feature[...] = jnp.zeros_like(feature)
    for kind, rows in enumerate((
        ((0, -2.0 * Q_SCALE * star_x), (3, Q_SCALE * (xx + softening)), (11, Q_SCALE * one)),
        ((0, -P_SCALE * star_v), (3, P_SCALE * xv), (4, -P_SCALE * star_x), (12, P_SCALE * one)),
        (
            (0, -G_SCALE * star_a), (3, G_SCALE * vv), (4, -2.0 * G_SCALE * star_v),
            (8, -G_SCALE * star_x), (13, G_SCALE * one),
        ),
    )):
        for row, value in rows:
            feature[kind, row : row + value.shape[0], :] = value
        high, middle, low = split3(feature[kind])
        weights[kind] = jnp.concatenate([high, middle, low, high, middle, high], axis=0)

    total[...] = jnp.zeros_like(total)
    total_low[...] = jnp.zeros_like(total_low)

    def chunk_of(number):
        return jnp.concatenate([slots[number * CHUNK + u] for u in range(CHUNK)], axis=1)

    def forward(rows, parity, kind, tile):
        columns = slice(tile * TILE, (tile + 1) * TILE)
        pairs[parity, kind, :, columns] = product(rows, weights[kind, :, columns], 0)

    for number in range(len(plan)):
        if plan[number][0] == -1 and due[number] == -1:
            copy(number).wait_recv()
    rows = source_rows(chunk_of(0))
    for kind in range(3):
        for tile in range(targets // TILE):
            forward(rows, 0, kind, tile)

    events = sorted(set([d for d in due if d >= 0] + [t[0] for t in plan if t[0] >= 0]))

    def branch(step, numbers):
        if len(numbers) <= 2:
            for number in numbers:
                pl.when(step == number)(functools.partial(exchange, number))
            return
        middle = len(numbers) // 2
        first, second = numbers[:middle], numbers[middle:]
        pl.when(step < second[0])(functools.partial(branch, step, first))
        pl.when(step >= second[0])(functools.partial(branch, step, second))

    def body(parts, numbers, step, carry):
        branch(step, numbers)
        for parity in range(parts):
            chunk = step * PARTS + parity
            now, later = parity % 2, (parity + 1) % 2
            fine, coarse = sum_rows(chunk_of(chunk))
            ahead = source_rows(chunk_of(lax.min(chunk + 1, BLOCKS // CHUNK - 1)))
            work = [(kind, tile) for tile in range(targets // TILE) for kind in range(3)]
            units = [(b, tile) for tile in range(targets // TILE) for b in range(CHUNK)]
            done = 0
            for place, (b, tile) in enumerate(units):
                js = slice(b * half, (b + 1) * half)
                columns = slice(tile * TILE, (tile + 1) * TILE)
                q, p, g = [pairs[now, kind, js, columns] for kind in range(3)]
                root = lax.rsqrt(q)
                inverse = pl.reciprocal(q, approx=True)
                w = inverse * root
                radial = p * inverse
                c1 = radial * w
                c2 = (w * inverse) * (p * radial - g)
                for kind, value in enumerate((w, c1, c2)):
                    high = value.astype(bf16)
                    low = (value - high.astype(f32)).astype(coarse[kind].dtype)
                    begin, end = FINE_ROWS[kind]
                    total[begin:end, columns] += product(fine[kind][:, js], high, 1)
                    total_low[kind, :, columns] += product(coarse[kind][:, js], low, 1)
                until = (place + 1) * len(work) // len(units)
                for kind, at in work[done:until]:
                    forward(ahead, later, kind, at)
                done = until
        return carry

    early = functools.partial(body, PARTS, [e for e in events if e < EARLY])
    lax.fori_loop(0, EARLY, early, 0)
    late = functools.partial(body, LATE_PARTS, [e for e in events if e >= EARLY])
    stride = LATE_PARTS // PARTS
    steps = (BLOCKS // STEP - EARLY) // stride
    lax.fori_loop(0, steps, lambda number, carry: late(EARLY + stride * number, carry), 0)

    sw = total[0:16] + total[16:32] + total_low[0, 0:16] + total_low[0, 16:32]
    s1 = total[32:40] + total[40:48] + total[48:56] + total_low[1, 0:8] + total_low[1, 16:24]
    s2 = (
        total[64:68] + total[68:72] + total[72:76]
        + total_low[2, 0:4] + total_low[2, 8:12] + total_low[2, 16:20]
    )
    share = 1.0 / (targets * BLOCKS)
    star_x, star_v, star_a = own[0:3, :], own[4:7, :], own[8:11, :]
    part[...] = jnp.zeros_like(part)
    part[0:3, :] = (W_BACK * share) * (sw[0:3] - star_x * sw[3:4])
    c1x = (C1_BACK * share) * (s1[0:3] - star_x * s1[3:4])
    part[3:6, :] = (W_BACK * share) * (sw[4:7] - star_v * sw[3:4]) - 3.0 * c1x
    part[6:9, :] = (
        (W_BACK * share) * (sw[8:11] - star_a * sw[3:4])
        - (6.0 * C1_BACK * share) * (s1[4:7] - star_v * s1[3:4])
        + (15.0 * C2_BACK * share) * (s2[0:3] - star_x * s2[3:4])
    )
    swap = pltpu.make_async_remote_copy(
        src_ref=part,
        dst_ref=other,
        send_sem=narrow_sem.at[0],
        recv_sem=narrow_sem.at[1],
        device_id=partner["narrow"],
        device_id_type=MESH,
    )
    swap.start()
    for number in range(len(plan)):
        copy(number).wait_send()
    swap.wait()
    results = correct(
        pos_ref[...], vel_ref[...], acc_ref[...], jerk_ref[...], snap_ref[...], part[...] + other[...]
    )
    for place, result in enumerate(results):
        out_ref[place] = result


def shards(positions, velocities, accelerations, jerks, snaps, masses):
    targets = positions.shape[1]
    half = targets // 2
    count = len(transfers())
    results = pl.pallas_call(
        forces_kernel,
        out_shape=jax.ShapeDtypeStruct((6, 3, targets), f32),
        in_specs=[pl.BlockSpec(memory_space=pltpu.HBM)] * 6,
        out_specs=pl.BlockSpec(memory_space=pltpu.VMEM),
        scratch_shapes=[pltpu.VMEM((3, targets), f32) for _ in range(5)]
        + [
            pltpu.VMEM((1, targets), f32),
            pltpu.VMEM((BLOCKS, 16, half), f32),
            pltpu.VMEM((16, targets), f32),
            pltpu.VMEM((3, 16, targets), f32),
            pltpu.VMEM((3, 96, targets), bf16),
            pltpu.VMEM((2, 3, CHUNK * half, targets), f32),
            pltpu.VMEM((80, targets), f32),
            pltpu.VMEM((3, 32, targets), f32),
            pltpu.VMEM((16, targets), f32),
            pltpu.VMEM((16, targets), f32),
            pltpu.SemaphoreType.REGULAR((2,)),
            pltpu.SemaphoreType.DMA((6,)),
            pltpu.SemaphoreType.DMA((count,)),
            pltpu.SemaphoreType.DMA((count,)),
            pltpu.SemaphoreType.DMA((2,)),
        ],
        compiler_params=pltpu.CompilerParams(
            collective_id=0, has_side_effects=True, vmem_limit_bytes=60 * 2**20
        ),
    )(positions, velocities, accelerations, jerks, snaps, masses.reshape(1, targets))
    return tuple(results[place] for place in range(6))


def solution(mesh):
    return jax.shard_map(
        shards,
        mesh=mesh,
        in_specs=(P(None, "wide"),) * 5 + (P("wide"),),
        out_specs=(P(None, "wide"),) * 6,
        check_vma=False,
    )
```
